128 devices in a mesh: fsdp: 8 (over y, x_lo), tensor: 16 (over x_hi, z, core).
Axes of the slice: x: 4 (x_hi: 2, x_lo: 2; x = x_hi * 2 + x_lo), y: 4, z: 4, core: 2. Of those that a mesh axis runs over, the one named last changes fastest.
Arguments:
- prompt: bfloat16 [1024, 16384], P('tensor', 'fsdp'), may hold values from -6 to 6
- decode_in: bfloat16 [128, 16384], P('tensor', 'fsdp'), may hold values from -6 to 6
- gate_weight: bfloat16 [16384, 26624], P(('fsdp', 'tensor')), may hold values from -0.046875 to 0.046875
- up_weight: bfloat16 [16384, 26624], P(('fsdp', 'tensor')), may hold values from -0.046875 to 0.046875
- down_weight: bfloat16 [26624, 16384], P(None, ('fsdp', 'tensor')), may hold values from -0.0390625 to 0.0390625
Outputs:
- prompt_out: bfloat16 [1024, 16384], P('tensor', 'fsdp')
- decoded: bfloat16 [128, 16384], P('tensor', 'fsdp')
The draws below stay inside these ranges and needn't reach their ends.
All inputs are finite; a program needn't handle non-finite values.
Results may differ from the reference program's by a relative error of at most 0.019.
Values may be sent and summed in bfloat16 or wider, within the bound.
No kernel may reach another device: no remote copies, remote signals or barrier semaphores. Data moves between devices by JAX's collectives and lax.ppermute only.
A program may use at most 192 MiB of HBM per device.

```python
import jax
import jax.numpy as jnp

D = 16384
FF = 26624
STEPS = 2
PROMPT = 1024
ROWS = 128


def steps_of(rng, extent, shards, low, top_value):
    factor_of, own = 1.0, jax.random.fold_in(rng, 6)
    for axis_at, blocks in shards:
        steps = jnp.exp(jax.random.uniform(jax.random.fold_in(own, axis_at), (blocks,), jnp.float32, low / len(shards), top_value / len(shards)))
        factor_of = factor_of * jnp.repeat(steps, extent[axis_at] // blocks).reshape([-1 if axis == axis_at else 1 for axis in range(len(extent))])
    return factor_of


def bell_draw(rng, extent, scale, bound, cuts=(), dtype=jnp.bfloat16):
    drawn = jax.random.normal(rng, extent, jnp.float32) * scale
    if len(cuts) > 0:
        drawn = steps_of(rng, extent, cuts, -0.22, 0.18) * drawn
    return jnp.clip(drawn, min=-bound, max=bound).astype(dtype)


def setup_inputs(seed: int = 0) -> dict:
    streams_of = jax.random.split(jax.random.key(seed), 6)
    return {
        "prompt": bell_draw(streams_of[0], (PROMPT, D), 1.0, 6.0, ((0, 16), (1, 8))),
        "decode_in": bell_draw(streams_of[1], (ROWS, D), 1.0, 6.0, ((0, 16), (1, 8))),
        "gate_weight": bell_draw(streams_of[2], (D, FF), D ** -0.5, 0.046875, ((0, 128),)),
        "up_weight": bell_draw(streams_of[3], (D, FF), D ** -0.5, 0.046875, ((0, 128),)),
        "down_weight": bell_draw(streams_of[4], (FF, D), FF ** -0.5, 0.0390625, ((1, 128),)),
    }


def gated_block(rows, gate_weight, up_weight, down_weight):
    gate = jnp.dot(rows, gate_weight, preferred_element_type=jnp.float32)
    upper = jnp.dot(rows, up_weight, preferred_element_type=jnp.float32)
    hidden = (jax.nn.silu(gate) * upper).astype(jnp.bfloat16)
    return jnp.dot(hidden, down_weight, preferred_element_type=jnp.float32)


def reference(prompt, decode_in, gate_weight, up_weight, down_weight):
    prompt_out = gated_block(prompt, gate_weight, up_weight, down_weight).astype(jnp.bfloat16)
    state = decode_in
    for turn in range(STEPS):
        update = gated_block(state, gate_weight, up_weight, down_weight)
        state = (state.astype(jnp.float32) + update).astype(jnp.bfloat16)
    return prompt_out, state
```

```python
import jax
import jax.numpy as jnp
from jax import lax
from jax.experimental import pallas as pl
from jax.experimental.pallas import tpu as pltpu
from jax.sharding import Mesh, PartitionSpec as P

STEPS = 2
SHIFTS = (0, 1, -1, 2)
FLIP = (0, 2, 1, 3)
LANES = 128
VMEM_LIMIT = 60 * 1024 * 1024
PLAN = (("z", "x", "y"), ("x", "y", "z"), ("y", "z", "x"))
RINGS = {"x": ("xl", "xh"), "y": ("y",), "z": ("z",)}


def ring_index(ring, place, core):
    if ring == "x":
        place = (place % 2) * 2 + place // 2
    return place * 2 + core


def ring_permute(value, ring, slot):
    pairs = []
    for core, sign in ((0, 1), (1, -1)):
        for place in range(4):
            target = (place + sign * SHIFTS[slot]) % 4
            pairs.append((ring_index(ring, place, core), ring_index(ring, target, core)))
    return lax.ppermute(value, RINGS[ring] + ("c",), pairs)


def core_swap(value):
    return lax.ppermute(value, "c", [(0, 1), (1, 0)])


def params():
    return pltpu.CompilerParams(vmem_limit_bytes=VMEM_LIMIT)


def smem():
    return pl.BlockSpec(memory_space=pltpu.SMEM)


def vmem():
    return pl.BlockSpec(memory_space=pltpu.VMEM)


def copy_cost(nbytes):
    return pl.CostEstimate(flops=0, bytes_accessed=int(2 * nbytes), transcendentals=0)


def pack_gate_up(where, gate, up, begin, width):
    rows = gate.shape[0]
    base = begin // (2 * width)
    step = rows // 4

    def body(where_ref, *rest):
        ins, outs = rest[:8], rest[8:]
        core = where_ref[0]
        for slot in range(4):
            for at in range(2):
                source = ins[4 * at + slot]
                outs[slot][0, at] = source[:, pl.ds(pl.multiple_of(core * width, LANES), width)]
                outs[slot][1, at] = source[:, pl.ds(pl.multiple_of((1 - core) * width, LANES), width)]

    def columns(slot):
        return lambda at, where_ref: (at, base + where_ref[1 + slot])

    return pl.pallas_call(
        body,
        out_shape=[jax.ShapeDtypeStruct((2, 2, rows, width), gate.dtype)] * 4,
        grid_spec=pltpu.PrefetchScalarGridSpec(
            num_scalar_prefetch=1,
            grid=(rows // step,),
            in_specs=[pl.BlockSpec((step, 2 * width), columns(slot)) for slot in range(4)] * 2,
            out_specs=[pl.BlockSpec((2, 2, step, width), lambda at, where_ref: (0, 0, at, 0))] * 4,
        ),
        compiler_params=params(),
        cost_estimate=copy_cost(16 * rows * width * 2),
        name="pack_gate_up",
    )(where, *([gate] * 4), *([up] * 4))


def pack_down(where, down, begin, width):
    columns = down.shape[1]
    base = begin // width
    tile = tile_of(width)
    tiles = width // tile

    def body(where_ref, *rest):
        ins, outs = rest[:8], rest[8:]
        for slot in range(4):
            outs[slot][0] = ins[2 * slot][...]
            outs[slot][1] = ins[2 * slot + 1][...]

    def half(slot, other):
        def block(at, where_ref):
            core = 1 - where_ref[0] if other else where_ref[0]
            return ((base + 2 * where_ref[1 + slot] + core) * tiles + at, 0)

        return block

    return pl.pallas_call(
        body,
        out_shape=[jax.ShapeDtypeStruct((2, width, columns), down.dtype)] * 4,
        grid_spec=pltpu.PrefetchScalarGridSpec(
            num_scalar_prefetch=1,
            grid=(tiles,),
            in_specs=[
                pl.BlockSpec((tile, columns), half(slot, other)) for slot in range(4) for other in (False, True)
            ],
            out_specs=[pl.BlockSpec((2, tile, columns), lambda at, where_ref: (0, at, 0))] * 4,
        ),
        compiler_params=params(),
        cost_estimate=copy_cost(8 * width * columns * 2),
        name="pack_down",
    )(where, *([down] * 8))


def tile_of(width):
    return width // 3 if width % 384 == 0 else width // 2


def gate_up_products(part, where, mine, others, weights):
    own_weights, other_weights = weights
    rows, own = mine[0].shape
    width = other_weights.shape[3]
    quarter = rows // 4
    depth = 8 * own
    tile = tile_of(width)

    def body(where_ref, *rest):
        mine_refs, others_ref, weight_refs, other_ref = rest[:4], rest[4], rest[5:9], rest[9]
        outs, joined, sums = rest[10:14], rest[14], rest[15]

        @pl.when((pl.program_id(0) == 0) & (pl.program_id(1) == 0))
        def _():
            for slot in range(4):
                joined[:, own * slot : own * (slot + 1)] = mine_refs[slot][...]
                joined[:, own * (4 + slot) : own * (5 + slot)] = others_ref[slot]

        weight = jnp.concatenate([ref[0, 0] for ref in weight_refs] + [other_ref[slot, 0] for slot in range(4)], axis=0)
        product = jnp.dot(joined[...], weight, preferred_element_type=jnp.float32)
        sums[...] = product.reshape(4, quarter, tile)
        for slot in range(4):
            outs[slot][0] = sums[where_ref[5 + slot]].astype(jnp.bfloat16)

    return pl.pallas_call(
        body,
        grid=(2, width // tile),
        out_shape=[jax.ShapeDtypeStruct((2, quarter, width), jnp.bfloat16)] * 4,
        in_specs=[smem()]
        + [pl.BlockSpec((rows, own), lambda g, j: (0, 0))] * 4
        + [pl.BlockSpec((4, rows, own), lambda g, j: (part, 0, 0))]
        + [pl.BlockSpec((1, 1, own, tile), lambda g, j: (0, g, 0, j))] * 4
        + [pl.BlockSpec((4, 1, own, tile), lambda g, j: (0, g, 0, j))],
        out_specs=[pl.BlockSpec((1, quarter, tile), lambda g, j: (g, 0, j))] * 4,
        scratch_shapes=[
            pltpu.VMEM((rows, depth), jnp.bfloat16),
            pltpu.VMEM((4, quarter, tile), jnp.float32),
        ],
        compiler_params=params(),
        cost_estimate=pl.CostEstimate(
            flops=4 * rows * depth * width,
            bytes_accessed=2 * (rows * depth + 2 * depth * width + 2 * rows * width),
            transcendentals=0,
        ),
        name="gate_up_products",
    )(where, *mine, others, *own_weights, other_weights)


def first_sums(where, terms, kept):
    _, quarter, width = terms[0].shape
    block = quarter // 4
    tile = tile_of(width)

    def body(where_ref, *rest):
        ins, outs, sums = rest[:4], rest[4:8], rest[8]
        total = ins[0][0].astype(jnp.float32)
        for ref in ins[1:]:
            total = total + ref[0].astype(jnp.float32)
        sums[...] = total.reshape(4, block, tile)
        for slot in range(4):
            outs[slot][0] = sums[where_ref[9 + slot]].astype(kept)

    return pl.pallas_call(
        body,
        grid=(2, width // tile),
        out_shape=[jax.ShapeDtypeStruct((2, block, width), kept)] * 4,
        in_specs=[smem()] + [pl.BlockSpec((1, quarter, tile), lambda g, j: (g, 0, j))] * 4,
        out_specs=[pl.BlockSpec((1, block, tile), lambda g, j: (g, 0, j))] * 4,
        scratch_shapes=[pltpu.VMEM((4, block, tile), jnp.float32)],
        compiler_params=params(),
        cost_estimate=pl.CostEstimate(
            flops=8 * quarter * width, bytes_accessed=20 * quarter * width, transcendentals=0
        ),
        name="first_sums",
    )(where, *terms)


def down_products(where, hidden, weights):
    _, block, width = hidden[0].shape
    rows = 16 * block
    own_weights, other_weights = weights
    own = other_weights.shape[2]
    blocks = 16 if rows <= 256 else 4
    chunk = blocks * block
    held = jnp.bfloat16 if block % 16 == 0 else jnp.float32

    def body(where_ref, *rest):
        hidden_refs, weight_refs, theirs_ref = rest[:4], rest[4:8], rest[8]
        outs, other_ref, joined = rest[9:13], rest[13], rest[14]
        for first in range(4):
            for second in range(4):
                row = where_ref[13 + first] * 4 + where_ref[17 + second]
                joined[row] = hidden_refs[first][second].astype(held)

        def step(at, carry):
            value = joined[pl.ds(at * blocks, blocks)].reshape(chunk, width).astype(jnp.bfloat16)
            span = pl.ds(pl.multiple_of(at * chunk, chunk), chunk)
            for slot in range(4):
                weight = jnp.concatenate([weight_refs[slot][0], theirs_ref[slot]], axis=1)
                product = jnp.dot(value, weight, preferred_element_type=jnp.float32)
                product = product.astype(jnp.bfloat16)
                outs[FLIP[slot]][span, :] = product[:, :own]
                other_ref[FLIP[slot], span, :] = product[:, own:]
            return carry

        lax.fori_loop(0, rows // chunk, step, 0)

    result = pl.pallas_call(
        body,
        grid=(1,),
        out_shape=[jax.ShapeDtypeStruct((rows, own), jnp.bfloat16)] * 4
        + [jax.ShapeDtypeStruct((4, rows, own), jnp.bfloat16)],
        in_specs=[smem()]
        + [vmem()] * 4
        + [pl.BlockSpec((1, width, own), lambda at: (0, 0, 0))] * 4
        + [vmem()],
        out_specs=[vmem()] * 5,
        scratch_shapes=[pltpu.VMEM((16, block, width), held)],
        compiler_params=params(),
        cost_estimate=pl.CostEstimate(
            flops=16 * rows * width * own,
            bytes_accessed=2 * (rows * width + 8 * width * own + 8 * rows * own),
            transcendentals=0,
        ),
        name="down_products",
    )(where, *hidden, *own_weights, other_weights)
    return result[:4], result[4]


def exchange(values, ring):
    return [values[0]] + [ring_permute(values[slot], ring, slot) for slot in (1, 2, 3)]


def gated(gate_sum, up_sum):
    return (jax.nn.silu(gate_sum) * up_sum).astype(jnp.bfloat16)


def gather_rows(rows):
    mine = [[rows, None, None, None] for _ in PLAN]
    for slot in (1, 2, 3):
        for at, (cross, _, _) in enumerate(PLAN):
            mine[at][slot] = ring_permute(rows, cross, slot)
    return mine


def exchange_all(values, rings):
    result = [[value[0], None, None, None] for value in values]
    first = [ring_permute(value[1], ring, 1) for value, ring in zip(values, rings)]
    later = lax.optimization_barrier([value[1:] for value in values])
    second = [ring_permute(value[1], ring, 2) for value, ring in zip(later, rings)]
    third, first = lax.optimization_barrier(([value[2] for value in later], first))
    third = [ring_permute(value, ring, 3) for value, ring in zip(third, rings)]
    return [[value[0], *slots] for value, *slots in zip(values, first, second, third)]


def share_cores(received):
    return received, core_swap(jnp.stack([value[1] for value in received]))


def block_update(mine, others, wheres, gate_up, down):
    rows = mine[0][0].shape[0]
    kept = jnp.bfloat16 if rows >= 256 else jnp.float32
    cross, first, second = zip(*PLAN)
    parts = [
        gate_up_products(at, where, mine[at], others, weights)
        for at, (where, weights) in enumerate(zip(wheres, gate_up))
    ]
    parts = exchange_all(parts, first)
    sums = [first_sums(where, terms, kept) for where, terms in zip(wheres, parts)]
    sums = exchange_all(sums, second)
    hidden = []
    for terms in sums:
        both = sum(term.astype(jnp.float32) for term in terms)
        hidden.append(gated(both[0], both[1]))
    hidden = exchange_all([[value] * 4 for value in hidden], second)
    hidden = exchange_all([[jnp.stack(value)] * 4 for value in hidden], first)
    terms, sent = [], []
    for where, value, weights in zip(wheres, hidden, down):
        products, other = down_products(where, value, weights)
        other = core_swap(other)
        pairs = [
            product.astype(jnp.float32) + other[slot].astype(jnp.float32) for slot, product in enumerate(products)
        ]
        terms.append(pairs[0])
        sent.append([pairs[0]] + [pair.astype(jnp.bfloat16) for pair in pairs[1:]])
    for received in exchange_all(sent, cross):
        terms += [term.astype(jnp.float32) for term in received[1:]]
    return sum(terms[1:], terms[0])


def shards(prompt, decode_in, gate_weight, up_weight, down_weight):
    core = lax.axis_index("c")
    sign = 1 - 2 * core
    place = {
        "x": lax.axis_index("xh") * 2 + lax.axis_index("xl"),
        "y": lax.axis_index("y"),
        "z": lax.axis_index("z"),
    }
    tensor = ("xh", "z", "c")
    own = down_weight.shape[1]

    units = gate_weight.shape[1] // (8 * LANES)
    widths = [(units // 3 + (1 if at < units % 3 else 0)) * LANES for at in range(3)]
    begins = [8 * sum(widths[:at]) for at in range(3)]

    wheres = []
    for cross, first, second in PLAN:
        to = lambda ring: [(place[ring] + sign * shift) % 4 for shift in SHIFTS]
        back = lambda ring: [(place[ring] - sign * shift) % 4 for shift in SHIFTS]
        where = [core] + to(cross) + to(first) + to(second) + back(first) + back(second)
        wheres.append(jnp.stack([jnp.asarray(entry, jnp.int32) for entry in where]))

    cross = [rings[0] for rings in PLAN]
    packing = list(zip(wheres, begins, widths))
    packed = [pack_gate_up(where, gate_weight, up_weight, *at) for where, *at in packing]
    received = exchange_all(packed, cross)

    count, decode_count = prompt.shape[0], decode_in.shape[0]
    block = count + decode_count
    both = jnp.concatenate([prompt, decode_in], axis=0)
    both = both.reshape(block, 16, own).swapaxes(0, 1)
    both = lax.all_to_all(both, tensor, split_axis=0, concat_axis=0, tiled=True)
    prompt_rows, state = both[:, :count], both[:, count:]

    packed = [pack_down(where, down_weight, *at) for where, *at in packing]
    gate_up = [share_cores(values) for values in received]
    received, packed = lax.optimization_barrier((received, packed))
    down = [share_cores(values) for values in exchange_all(packed, cross)]

    span = count // STEPS
    outs = []
    for turn in range(STEPS):
        rows = jnp.concatenate([prompt_rows[:, turn * span : (turn + 1) * span], state], axis=1)
        mine = gather_rows(rows.reshape(-1, own))
        others = core_swap(jnp.stack([value for part in mine for value in part]))
        update = block_update(mine, others, wheres, gate_up, down).reshape(rows.shape)
        outs.append(update[:, :span].astype(jnp.bfloat16))
        state = (state.astype(jnp.float32) + update[:, span:]).astype(jnp.bfloat16)

    both = jnp.concatenate(outs + [state], axis=1)
    both = lax.all_to_all(both, tensor, split_axis=0, concat_axis=0, tiled=True)
    both = both.swapaxes(0, 1).reshape(block, 16 * own)
    return both[:count], both[count:]


def solution(mesh):
    fine = Mesh(mesh.devices.reshape(4, 2, 2, 4, 2), ("y", "xl", "xh", "z", "c"))
    fsdp, tensor = ("y", "xl"), ("xh", "z", "c")
    return jax.shard_map(
        shards,
        mesh=fine,
        in_specs=(
            P(tensor, fsdp),
            P(tensor, fsdp),
            P(fsdp + tensor, None),
            P(fsdp + tensor, None),
            P(None, fsdp + tensor),
        ),
        out_specs=(P(tensor, fsdp), P(tensor, fsdp)),
        check_vma=False,
    )
```

```python
import jax
import jax.numpy as jnp
from jax import lax
from jax.experimental import pallas as pl
from jax.experimental.pallas import tpu as pltpu
from jax.sharding import Mesh, PartitionSpec as P

STEPS = 2
SHIFTS = (0, 1, -1, 2)
FLIP = (0, 2, 1, 3)
LANES = 128
VMEM_LIMIT = 60 * 1024 * 1024
PLAN = (("z", "x", "y"), ("x", "y", "z"), ("y", "z", "x"))
RINGS = {"x": ("xl", "xh"), "y": ("y",), "z": ("z",)}


def ring_index(ring, place, core):
    if ring == "x":
        place = (place % 2) * 2 + place // 2
    return place * 2 + core


def ring_permute(value, ring, slot):
    pairs = []
    for core, sign in ((0, 1), (1, -1)):
        for place in range(4):
            target = (place + sign * SHIFTS[slot]) % 4
            pairs.append((ring_index(ring, place, core), ring_index(ring, target, core)))
    return lax.ppermute(value, RINGS[ring] + ("c",), pairs)


def core_swap(value):
    return lax.ppermute(value, "c", [(0, 1), (1, 0)])


def params():
    return pltpu.CompilerParams(vmem_limit_bytes=VMEM_LIMIT)


def smem():
    return pl.BlockSpec(memory_space=pltpu.SMEM)


def vmem():
    return pl.BlockSpec(memory_space=pltpu.VMEM)


def copy_cost(nbytes):
    return pl.CostEstimate(flops=0, bytes_accessed=int(2 * nbytes), transcendentals=0)


def pack_gate_up(where, gate, up, begin, width):
    rows = gate.shape[0]
    base = begin // (2 * width)
    step = rows // 4

    def body(where_ref, *rest):
        ins, outs = rest[:8], rest[8:]
        core = where_ref[0]
        for slot in range(4):
            for at in range(2):
                source = ins[4 * at + slot]
                outs[slot][0, at] = source[:, pl.ds(pl.multiple_of(core * width, LANES), width)]
                outs[slot][1, at] = source[:, pl.ds(pl.multiple_of((1 - core) * width, LANES), width)]

    def columns(slot):
        return lambda at, where_ref: (at, base + where_ref[1 + slot])

    return pl.pallas_call(
        body,
        out_shape=[jax.ShapeDtypeStruct((2, 2, rows, width), gate.dtype)] * 4,
        grid_spec=pltpu.PrefetchScalarGridSpec(
            num_scalar_prefetch=1,
            grid=(rows // step,),
            in_specs=[pl.BlockSpec((step, 2 * width), columns(slot)) for slot in range(4)] * 2,
            out_specs=[pl.BlockSpec((2, 2, step, width), lambda at, where_ref: (0, 0, at, 0))] * 4,
        ),
        compiler_params=params(),
        cost_estimate=copy_cost(16 * rows * width * 2),
        name="pack_gate_up",
    )(where, *([gate] * 4), *([up] * 4))


def pack_down(where, down, begin, width):
    columns = down.shape[1]
    base = begin // width
    tiles = 2
    tile = width // tiles

    def body(where_ref, *rest):
        ins, outs = rest[:8], rest[8:]
        for slot in range(4):
            outs[slot][0] = ins[2 * slot][...]
            outs[slot][1] = ins[2 * slot + 1][...]

    def half(slot, other):
        def block(at, where_ref):
            core = 1 - where_ref[0] if other else where_ref[0]
            return ((base + 2 * where_ref[1 + slot] + core) * tiles + at, 0)

        return block

    return pl.pallas_call(
        body,
        out_shape=[jax.ShapeDtypeStruct((2, width, columns), down.dtype)] * 4,
        grid_spec=pltpu.PrefetchScalarGridSpec(
            num_scalar_prefetch=1,
            grid=(tiles,),
            in_specs=[
                pl.BlockSpec((tile, columns), half(slot, other)) for slot in range(4) for other in (False, True)
            ],
            out_specs=[pl.BlockSpec((2, tile, columns), lambda at, where_ref: (0, at, 0))] * 4,
        ),
        compiler_params=params(),
        cost_estimate=copy_cost(8 * width * columns * 2),
        name="pack_down",
    )(where, *([down] * 8))


def tile_of(width):
    return width


def gate_up_products(where, mine, weights):
    own_weights, other_weights = weights
    _, rows, own = mine[0].shape
    width = other_weights.shape[3]
    quarter = rows // 4
    depth = 8 * own
    tile = tile_of(width)

    def body(where_ref, *rest):
        mine_refs, weight_refs, other_ref = rest[:4], rest[4:8], rest[8]
        outs, joined, sums = rest[9:13], rest[13], rest[14]

        @pl.when((pl.program_id(0) == 0) & (pl.program_id(1) == 0))
        def _():
            for slot in range(4):
                joined[:, own * slot : own * (slot + 1)] = mine_refs[slot][0]
                joined[:, own * (4 + slot) : own * (5 + slot)] = mine_refs[FLIP[slot]][1]

        weight = jnp.concatenate([ref[0, 0] for ref in weight_refs] + [other_ref[slot, 0] for slot in range(4)], axis=0)
        product = jnp.dot(joined[...], weight, preferred_element_type=jnp.float32)
        sums[...] = product.reshape(4, quarter, tile)
        for slot in range(4):
            outs[slot][0] = sums[where_ref[5 + slot]].astype(jnp.bfloat16)

    return pl.pallas_call(
        body,
        grid=(2, width // tile),
        out_shape=[jax.ShapeDtypeStruct((2, quarter, width), jnp.bfloat16)] * 4,
        in_specs=[smem()]
        + [pl.BlockSpec((2, rows, own), lambda g, j: (0, 0, 0))] * 4
        + [pl.BlockSpec((1, 1, own, tile), lambda g, j: (0, g, 0, j))] * 4
        + [pl.BlockSpec((4, 1, own, tile), lambda g, j: (0, g, 0, j))],
        out_specs=[pl.BlockSpec((1, quarter, tile), lambda g, j: (g, 0, j))] * 4,
        scratch_shapes=[
            pltpu.VMEM((rows, depth), jnp.bfloat16),
            pltpu.VMEM((4, quarter, tile), jnp.float32),
        ],
        compiler_params=params(),
        cost_estimate=pl.CostEstimate(
            flops=4 * rows * depth * width,
            bytes_accessed=2 * (rows * depth + 2 * depth * width + 2 * rows * width),
            transcendentals=0,
        ),
        name="gate_up_products",
    )(where, *mine, *own_weights, other_weights)


def first_sums(where, terms, kept):
    _, quarter, width = terms[0].shape
    block = quarter // 4
    tile = tile_of(width)

    def body(where_ref, *rest):
        ins, outs, sums = rest[:4], rest[4:8], rest[8]
        total = ins[0][0].astype(jnp.float32)
        for ref in ins[1:]:
            total = total + ref[0].astype(jnp.float32)
        sums[...] = total.reshape(4, block, tile)
        for slot in range(4):
            outs[slot][0] = sums[where_ref[9 + slot]].astype(kept)

    return pl.pallas_call(
        body,
        grid=(2, width // tile),
        out_shape=[jax.ShapeDtypeStruct((2, block, width), kept)] * 4,
        in_specs=[smem()] + [pl.BlockSpec((1, quarter, tile), lambda g, j: (g, 0, j))] * 4,
        out_specs=[pl.BlockSpec((1, block, tile), lambda g, j: (g, 0, j))] * 4,
        scratch_shapes=[pltpu.VMEM((4, block, tile), jnp.float32)],
        compiler_params=params(),
        cost_estimate=pl.CostEstimate(
            flops=8 * quarter * width, bytes_accessed=20 * quarter * width, transcendentals=0
        ),
        name="first_sums",
    )(where, *terms)


def down_products(where, hidden, weights):
    _, block, width = hidden[0].shape
    rows = 16 * block
    own_weights, other_weights = weights
    own = other_weights.shape[2]
    blocks = 16 if rows <= 256 else 4
    chunk = blocks * block
    held = jnp.bfloat16 if block % 16 == 0 else jnp.float32

    def body(where_ref, *rest):
        hidden_refs, weight_refs, theirs_ref = rest[:4], rest[4:8], rest[8]
        outs, other_ref, joined = rest[9:13], rest[13], rest[14]
        for first in range(4):
            for second in range(4):
                row = where_ref[13 + first] * 4 + where_ref[17 + second]
                joined[row] = hidden_refs[first][second].astype(held)

        def step(at, carry):
            value = joined[pl.ds(at * blocks, blocks)].reshape(chunk, width).astype(jnp.bfloat16)
            span = pl.ds(pl.multiple_of(at * chunk, chunk), chunk)
            for slot in range(4):
                weight = jnp.concatenate([weight_refs[slot][0], theirs_ref[slot]], axis=1)
                product = jnp.dot(value, weight, preferred_element_type=jnp.float32)
                product = product.astype(jnp.bfloat16)
                outs[FLIP[slot]][span, :] = product[:, :own]
                other_ref[FLIP[slot], span, :] = product[:, own:]
            return carry

        lax.fori_loop(0, rows // chunk, step, 0)

    result = pl.pallas_call(
        body,
        grid=(1,),
        out_shape=[jax.ShapeDtypeStruct((rows, own), jnp.bfloat16)] * 4
        + [jax.ShapeDtypeStruct((4, rows, own), jnp.bfloat16)],
        in_specs=[smem()]
        + [vmem()] * 4
        + [pl.BlockSpec((1, width, own), lambda at: (0, 0, 0))] * 4
        + [vmem()],
        out_specs=[vmem()] * 5,
        scratch_shapes=[pltpu.VMEM((16, block, width), held)],
        compiler_params=params(),
        cost_estimate=pl.CostEstimate(
            flops=16 * rows * width * own,
            bytes_accessed=2 * (rows * width + 8 * width * own + 8 * rows * own),
            transcendentals=0,
        ),
        name="down_products",
    )(where, *hidden, *own_weights, other_weights)
    return result[:4], result[4]


def exchange(values, ring):
    return [values[0]] + [ring_permute(values[slot], ring, slot) for slot in (1, 2, 3)]


def gated(gate_sum, up_sum):
    return (jax.nn.silu(gate_sum) * up_sum).astype(jnp.bfloat16)


def core_pair(rows):
    return jnp.stack([rows, core_swap(rows)])


def gather_rows(rows):
    pair = core_pair(rows)
    mine = [[pair, None, None, None] for _ in PLAN]
    for slot in (1, 2, 3):
        for at, (cross, _, _) in enumerate(PLAN):
            mine[at][slot] = ring_permute(pair, cross, slot)
    return mine


def exchange_all(values, rings):
    first = [ring_permute(value[1], ring, 1) for value, ring in zip(values, rings)]
    later = lax.optimization_barrier([value[1:] for value in values])
    second = [ring_permute(value[1], ring, 2) for value, ring in zip(later, rings)]
    third, first = lax.optimization_barrier(([value[2] for value in later], first))
    third = [ring_permute(value, ring, 3) for value, ring in zip(third, rings)]
    return [[value[0], *slots] for value, *slots in zip(values, first, second, third)]


def in_turn(steps, ring, flying=2):
    results = []
    for value, slot in steps:
        if len(results) >= flying:
            value, results[-flying] = lax.optimization_barrier((value, results[-flying]))
        results.append(ring_permute(value, ring, slot))
    return results


def share_cores(received):
    return received, core_swap(jnp.stack([value[1] for value in received]))


def block_update(mine, wheres, gate_up, down):
    rows = mine[0][0].shape[1]
    kept = jnp.bfloat16 if rows >= 256 else jnp.float32
    cross, first, second = zip(*PLAN)
    parts = [
        gate_up_products(where, values, weights) for where, values, weights in zip(wheres, mine, gate_up)
    ]
    parts = exchange_all(parts, first)
    sums = [first_sums(where, terms, kept) for where, terms in zip(wheres, parts)]
    sums = exchange_all(sums, second)
    hidden = []
    for terms in sums:
        both = sum(term.astype(jnp.float32) for term in terms)
        hidden.append(gated(both[0], both[1]))
    hidden = exchange_all([[value] * 4 for value in hidden], second)
    hidden = exchange_all([[jnp.stack(value)] * 4 for value in hidden], first)
    terms, sent = [], []
    for where, value, weights in zip(wheres, hidden, down):
        products, other = down_products(where, value, weights)
        other = core_swap(other)
        pairs = [
            product.astype(jnp.float32) + other[slot].astype(jnp.float32) for slot, product in enumerate(products)
        ]
        terms.append(pairs[0])
        sent.append([pairs[0]] + [pair.astype(jnp.bfloat16) for pair in pairs[1:]])
    for received in exchange_all(sent, cross):
        terms += [term.astype(jnp.float32) for term in received[1:]]
    return sum(terms[1:], terms[0])


def shards(prompt, decode_in, gate_weight, up_weight, down_weight):
    core = lax.axis_index("c")
    sign = 1 - 2 * core
    place = {
        "x": lax.axis_index("xh") * 2 + lax.axis_index("xl"),
        "y": lax.axis_index("y"),
        "z": lax.axis_index("z"),
    }
    tensor = ("xh", "z", "c")
    own = down_weight.shape[1]

    units, parts = gate_weight.shape[1] // (8 * LANES), len(PLAN)
    widths = [(units // parts + (1 if at < units % parts else 0)) * LANES for at in range(parts)]
    begins = [8 * sum(widths[:at]) for at in range(parts)]

    wheres = []
    for cross, first, second in PLAN:
        to = lambda ring: [(place[ring] + sign * shift) % 4 for shift in SHIFTS]
        back = lambda ring: [(place[ring] - sign * shift) % 4 for shift in SHIFTS]
        where = [core] + to(cross) + to(first) + to(second) + back(first) + back(second)
        wheres.append(jnp.stack([jnp.asarray(entry, jnp.int32) for entry in where]))

    cross = [rings[0] for rings in PLAN]
    packing = list(zip(wheres, begins, widths))
    packed = [pack_gate_up(where, gate_weight, up_weight, *at) for where, *at in packing]
    packed_down = [pack_down(where, down_weight, *at) for where, *at in packing]
    weights = [
        in_turn([(gates[slot], slot) for slot in (1, 2, 3)] + [(downs[slot], slot) for slot in (1, 2, 3)], ring)
        for ring, gates, downs in zip(cross, packed, packed_down)
    ]

    prompt, decode_in, weights[0][0] = lax.optimization_barrier((prompt, decode_in, weights[0][0]))
    count, decode_count = prompt.shape[0], decode_in.shape[0]
    block, span = count + decode_count, count // STEPS
    both = jnp.concatenate([prompt, decode_in], axis=0)
    both = both.reshape(block, 16, own).swapaxes(0, 1)
    both = lax.all_to_all(both, tensor, split_axis=0, concat_axis=0, tiled=True)
    prompt_rows, state = both[:, :count], both[:, count:]

    def turn_rows(turn):
        return jnp.concatenate([prompt_rows[:, turn * span : (turn + 1) * span], state], axis=1)

    rows = turn_rows(0)
    pair = core_pair(rows.reshape(-1, own))
    mine = [[pair, *in_turn([(pair, slot) for slot in (1, 2, 3)], ring, 1)] for ring in cross]
    gate_up = [share_cores([gates[0], *results[:3]]) for gates, results in zip(packed, weights)]
    down = [share_cores([downs[0], *results[3:]]) for downs, results in zip(packed_down, weights)]

    outs = []
    for turn in range(STEPS):
        if turn > 0:
            rows = turn_rows(turn)
            mine = gather_rows(rows.reshape(-1, own))
        update = block_update(mine, wheres, gate_up, down).reshape(rows.shape)
        outs.append(update[:, :span].astype(jnp.bfloat16))
        state = (state.astype(jnp.float32) + update[:, span:]).astype(jnp.bfloat16)

    both = jnp.concatenate(outs + [state], axis=1)
    both = lax.all_to_all(both, tensor, split_axis=0, concat_axis=0, tiled=True)
    both = both.swapaxes(0, 1).reshape(block, 16 * own)
    return both[:count], both[count:]


def solution(mesh):
    fine = Mesh(mesh.devices.reshape(4, 2, 2, 4, 2), ("y", "xl", "xh", "z", "c"))
    fsdp, tensor = ("y", "xl"), ("xh", "z", "c")
    return jax.shard_map(
        shards,
        mesh=fine,
        in_specs=(
            P(tensor, fsdp),
            P(tensor, fsdp),
            P(fsdp + tensor, None),
            P(fsdp + tensor, None),
            P(None, fsdp + tensor),
        ),
        out_specs=(P(tensor, fsdp), P(tensor, fsdp)),
        check_vma=False,
    )
```

```python
import jax
import jax.numpy as jnp
from jax import lax
from jax.experimental import pallas as pl
from jax.experimental.pallas import tpu as pltpu
from jax.sharding import Mesh, PartitionSpec as P

STEPS = 2
SHIFTS = (0, 1, -1, 2)
FLIP = (0, 2, 1, 3)
LANES = 128
VMEM_LIMIT = 60 * 1024 * 1024
PLAN = (("z", "x", "y"), ("x", "y", "z"), ("y", "z", "x"))
RINGS = {"x": ("xl", "xh"), "y": ("y",), "z": ("z",)}


def ring_index(ring, place, core):
    if ring == "x":
        place = (place % 2) * 2 + place // 2
    return place * 2 + core


def ring_permute(value, ring, slot):
    pairs = []
    for core, sign in ((0, 1), (1, -1)):
        for place in range(4):
            target = (place + sign * SHIFTS[slot]) % 4
            pairs.append((ring_index(ring, place, core), ring_index(ring, target, core)))
    return lax.ppermute(value, RINGS[ring] + ("c",), pairs)


def core_swap(value):
    return lax.ppermute(value, "c", [(0, 1), (1, 0)])


def params():
    return pltpu.CompilerParams(vmem_limit_bytes=VMEM_LIMIT)


def smem():
    return pl.BlockSpec(memory_space=pltpu.SMEM)


def vmem():
    return pl.BlockSpec(memory_space=pltpu.VMEM)


def copy_cost(nbytes):
    return pl.CostEstimate(flops=0, bytes_accessed=int(2 * nbytes), transcendentals=0)


def pack_gate_up(where, gate, up, begin, width):
    rows = gate.shape[0]
    base = begin // (2 * width)
    step = rows // 4

    def body(where_ref, *rest):
        ins, outs = rest[:8], rest[8:]
        core = where_ref[0]
        for slot in range(4):
            for at in range(2):
                source = ins[4 * at + slot]
                outs[slot][0, at] = source[:, pl.ds(pl.multiple_of(core * width, LANES), width)]
                outs[slot][1, at] = source[:, pl.ds(pl.multiple_of((1 - core) * width, LANES), width)]

    def columns(slot):
        return lambda at, where_ref: (at, base + where_ref[1 + slot])

    return pl.pallas_call(
        body,
        out_shape=[jax.ShapeDtypeStruct((2, 2, rows, width), gate.dtype)] * 4,
        grid_spec=pltpu.PrefetchScalarGridSpec(
            num_scalar_prefetch=1,
            grid=(rows // step,),
            in_specs=[pl.BlockSpec((step, 2 * width), columns(slot)) for slot in range(4)] * 2,
            out_specs=[pl.BlockSpec((2, 2, step, width), lambda at, where_ref: (0, 0, at, 0))] * 4,
        ),
        compiler_params=params(),
        cost_estimate=copy_cost(16 * rows * width * 2),
        name="pack_gate_up",
    )(where, *([gate] * 4), *([up] * 4))


def pack_down(where, down, begin, width):
    columns = down.shape[1]
    base = begin // width
    tiles = 2
    tile = width // tiles

    def body(where_ref, *rest):
        ins, outs = rest[:8], rest[8:]
        for slot in range(4):
            outs[slot][0] = ins[2 * slot][...]
            outs[slot][1] = ins[2 * slot + 1][...]

    def half(slot, other):
        def block(at, where_ref):
            core = 1 - where_ref[0] if other else where_ref[0]
            return ((base + 2 * where_ref[1 + slot] + core) * tiles + at, 0)

        return block

    return pl.pallas_call(
        body,
        out_shape=[jax.ShapeDtypeStruct((2, width, columns), down.dtype)] * 4,
        grid_spec=pltpu.PrefetchScalarGridSpec(
            num_scalar_prefetch=1,
            grid=(tiles,),
            in_specs=[
                pl.BlockSpec((tile, columns), half(slot, other)) for slot in range(4) for other in (False, True)
            ],
            out_specs=[pl.BlockSpec((2, tile, columns), lambda at, where_ref: (0, at, 0))] * 4,
        ),
        compiler_params=params(),
        cost_estimate=copy_cost(8 * width * columns * 2),
        name="pack_down",
    )(where, *([down] * 8))


def tile_of(width):
    return width


def gate_up_products(where, mine, weights):
    own_weights, other_weights = weights
    _, rows, own = mine[0].shape
    width = other_weights.shape[3]
    quarter = rows // 4
    depth = 8 * own
    tile = tile_of(width)

    def body(where_ref, *rest):
        mine_refs, weight_refs, other_ref = rest[:4], rest[4:8], rest[8]
        outs, joined, sums = rest[9:13], rest[13], rest[14]

        @pl.when((pl.program_id(0) == 0) & (pl.program_id(1) == 0))
        def _():
            for slot in range(4):
                joined[:, own * slot : own * (slot + 1)] = mine_refs[slot][0]
                joined[:, own * (4 + slot) : own * (5 + slot)] = mine_refs[FLIP[slot]][1]

        weight = jnp.concatenate([ref[0, 0] for ref in weight_refs] + [other_ref[slot, 0] for slot in range(4)], axis=0)
        product = jnp.dot(joined[...], weight, preferred_element_type=jnp.float32)
        sums[...] = product.reshape(4, quarter, tile)
        for slot in range(4):
            outs[slot][0] = sums[where_ref[5 + slot]].astype(jnp.bfloat16)

    return pl.pallas_call(
        body,
        grid=(2, width // tile),
        out_shape=[jax.ShapeDtypeStruct((2, quarter, width), jnp.bfloat16)] * 4,
        in_specs=[smem()]
        + [pl.BlockSpec((2, rows, own), lambda g, j: (0, 0, 0))] * 4
        + [pl.BlockSpec((1, 1, own, tile), lambda g, j: (0, g, 0, j))] * 4
        + [pl.BlockSpec((4, 1, own, tile), lambda g, j: (0, g, 0, j))],
        out_specs=[pl.BlockSpec((1, quarter, tile), lambda g, j: (g, 0, j))] * 4,
        scratch_shapes=[
            pltpu.VMEM((rows, depth), jnp.bfloat16),
            pltpu.VMEM((4, quarter, tile), jnp.float32),
        ],
        compiler_params=params(),
        cost_estimate=pl.CostEstimate(
            flops=4 * rows * depth * width,
            bytes_accessed=2 * (rows * depth + 2 * depth * width + 2 * rows * width),
            transcendentals=0,
        ),
        name="gate_up_products",
    )(where, *mine, *own_weights, other_weights)


def first_sums(where, terms, kept):
    _, quarter, width = terms[0].shape
    block = quarter // 4
    tile = tile_of(width)

    def body(where_ref, *rest):
        ins, outs, sums = rest[:4], rest[4:8], rest[8]
        total = ins[0][0].astype(jnp.float32)
        for ref in ins[1:]:
            total = total + ref[0].astype(jnp.float32)
        sums[...] = total.reshape(4, block, tile)
        for slot in range(4):
            outs[slot][0] = sums[where_ref[9 + slot]].astype(kept)

    return pl.pallas_call(
        body,
        grid=(2, width // tile),
        out_shape=[jax.ShapeDtypeStruct((2, block, width), kept)] * 4,
        in_specs=[smem()] + [pl.BlockSpec((1, quarter, tile), lambda g, j: (g, 0, j))] * 4,
        out_specs=[pl.BlockSpec((1, block, tile), lambda g, j: (g, 0, j))] * 4,
        scratch_shapes=[pltpu.VMEM((4, block, tile), jnp.float32)],
        compiler_params=params(),
        cost_estimate=pl.CostEstimate(
            flops=8 * quarter * width, bytes_accessed=20 * quarter * width, transcendentals=0
        ),
        name="first_sums",
    )(where, *terms)


def down_products(where, hidden, weights):
    _, block, width = hidden[0].shape
    rows = 16 * block
    own_weights, other_weights = weights
    own = other_weights.shape[2]
    blocks = 16 if rows <= 256 else 4
    chunk = blocks * block
    held = jnp.bfloat16 if block % 16 == 0 else jnp.float32

    def body(where_ref, *rest):
        hidden_refs, weight_refs, theirs_ref = rest[:4], rest[4:8], rest[8]
        outs, other_ref, joined = rest[9:13], rest[13], rest[14]
        for first in range(4):
            for second in range(4):
                row = where_ref[13 + first] * 4 + where_ref[17 + second]
                joined[row] = hidden_refs[first][second].astype(held)

        def step(at, carry):
            value = joined[pl.ds(at * blocks, blocks)].reshape(chunk, width).astype(jnp.bfloat16)
            span = pl.ds(pl.multiple_of(at * chunk, chunk), chunk)
            for slot in range(4):
                weight = jnp.concatenate([weight_refs[slot][0], theirs_ref[slot]], axis=1)
                product = jnp.dot(value, weight, preferred_element_type=jnp.float32)
                product = product.astype(jnp.bfloat16)
                outs[FLIP[slot]][span, :] = product[:, :own]
                other_ref[FLIP[slot], span, :] = product[:, own:]
            return carry

        lax.fori_loop(0, rows // chunk, step, 0)

    result = pl.pallas_call(
        body,
        grid=(1,),
        out_shape=[jax.ShapeDtypeStruct((rows, own), jnp.bfloat16)] * 4
        + [jax.ShapeDtypeStruct((4, rows, own), jnp.bfloat16)],
        in_specs=[smem()]
        + [vmem()] * 4
        + [pl.BlockSpec((1, width, own), lambda at: (0, 0, 0))] * 4
        + [vmem()],
        out_specs=[vmem()] * 5,
        scratch_shapes=[pltpu.VMEM((16, block, width), held)],
        compiler_params=params(),
        cost_estimate=pl.CostEstimate(
            flops=16 * rows * width * own,
            bytes_accessed=2 * (rows * width + 8 * width * own + 8 * rows * own),
            transcendentals=0,
        ),
        name="down_products",
    )(where, *hidden, *own_weights, other_weights)
    return result[:4], result[4]


def exchange(values, ring):
    return [values[0]] + [ring_permute(values[slot], ring, slot) for slot in (1, 2, 3)]


def gated(gate_sum, up_sum):
    return (jax.nn.silu(gate_sum) * up_sum).astype(jnp.bfloat16)


def core_pair(rows):
    return jnp.stack([rows, core_swap(rows)])


def gather_rows(rows):
    pair = core_pair(rows)
    mine = [[pair, None, None, None] for _ in PLAN]
    for slot in (1, 2, 3):
        for at, (cross, _, _) in enumerate(PLAN):
            mine[at][slot] = ring_permute(pair, cross, slot)
    return mine


def exchange_all(values, rings):
    first = [ring_permute(value[1], ring, 1) for value, ring in zip(values, rings)]
    later = lax.optimization_barrier([value[1:] for value in values])
    second = [ring_permute(value[1], ring, 2) for value, ring in zip(later, rings)]
    third, first = lax.optimization_barrier(([value[2] for value in later], first))
    third = [ring_permute(value, ring, 3) for value, ring in zip(third, rings)]
    return [[value[0], *slots] for value, *slots in zip(values, first, second, third)]


def in_turn(steps, ring, flying=2):
    results = []
    for value, slot in steps:
        if len(results) >= flying:
            value, results[-flying] = lax.optimization_barrier((value, results[-flying]))
        results.append(ring_permute(value, ring, slot))
    return results


def other_halves(received):
    _, parts, *rest = received[0].shape
    part, zeros = parts // 2, (0,) * len(rest)

    def body(*refs):
        for slot in range(4):
            refs[4][slot] = refs[slot][0]

    return pl.pallas_call(
        body,
        grid=(2,),
        out_shape=jax.ShapeDtypeStruct((4, parts, *rest), received[0].dtype),
        in_specs=[pl.BlockSpec((1, part, *rest), lambda at: (1, at, *zeros))] * 4,
        out_specs=pl.BlockSpec((4, part, *rest), lambda at: (0, at, *zeros)),
        compiler_params=params(),
        cost_estimate=copy_cost(4 * received[0].size),
        name="other_halves",
    )(*received)


def share_cores(received):
    return received, core_swap(other_halves(received))


def block_update(mine, wheres, gate_up, down):
    rows = mine[0][0].shape[1]
    kept = jnp.bfloat16 if rows >= 256 else jnp.float32
    cross, first, second = zip(*PLAN)
    parts = [
        gate_up_products(where, values, weights) for where, values, weights in zip(wheres, mine, gate_up)
    ]
    parts = exchange_all(parts, first)
    sums = [first_sums(where, terms, kept) for where, terms in zip(wheres, parts)]
    sums = exchange_all(sums, second)
    hidden = []
    for terms in sums:
        both = sum(term.astype(jnp.float32) for term in terms)
        hidden.append(gated(both[0], both[1]))
    hidden = exchange_all([[value] * 4 for value in hidden], second)
    hidden = exchange_all([[jnp.stack(value)] * 4 for value in hidden], first)
    terms, sent = [], []
    for where, value, weights in zip(wheres, hidden, down):
        products, other = down_products(where, value, weights)
        other = core_swap(other)
        pairs = [
            product.astype(jnp.float32) + other[slot].astype(jnp.float32) for slot, product in enumerate(products)
        ]
        terms.append(pairs[0])
        sent.append([pairs[0]] + [pair.astype(jnp.bfloat16) for pair in pairs[1:]])
    for received in exchange_all(sent, cross):
        terms += [term.astype(jnp.float32) for term in received[1:]]
    return sum(terms[1:], terms[0])


def shards(prompt, decode_in, gate_weight, up_weight, down_weight):
    core = lax.axis_index("c")
    sign = 1 - 2 * core
    place = {
        "x": lax.axis_index("xh") * 2 + lax.axis_index("xl"),
        "y": lax.axis_index("y"),
        "z": lax.axis_index("z"),
    }
    tensor = ("xh", "z", "c")
    own = down_weight.shape[1]

    units, parts = gate_weight.shape[1] // (8 * LANES), len(PLAN)
    widths = [(units // parts + (1 if at < units % parts else 0)) * LANES for at in range(parts)]
    begins = [8 * sum(widths[:at]) for at in range(parts)]

    wheres = []
    for cross, first, second in PLAN:
        to = lambda ring: [(place[ring] + sign * shift) % 4 for shift in SHIFTS]
        back = lambda ring: [(place[ring] - sign * shift) % 4 for shift in SHIFTS]
        where = [core] + to(cross) + to(first) + to(second) + back(first) + back(second)
        wheres.append(jnp.stack([jnp.asarray(entry, jnp.int32) for entry in where]))

    cross = [rings[0] for rings in PLAN]
    packing = list(zip(wheres, begins, widths))
    packed = [pack_gate_up(where, gate_weight, up_weight, *at) for where, *at in packing]
    packed_down = [pack_down(where, down_weight, *at) for where, *at in packing]
    weights = [
        in_turn([(gates[slot], slot) for slot in (1, 2, 3)] + [(downs[slot], slot) for slot in (1, 2, 3)], ring)
        for ring, gates, downs in zip(cross, packed, packed_down)
    ]

    prompt, decode_in, weights[0][0] = lax.optimization_barrier((prompt, decode_in, weights[0][0]))
    count, decode_count = prompt.shape[0], decode_in.shape[0]
    block, span = count + decode_count, count // STEPS
    both = jnp.concatenate([prompt, decode_in], axis=0)
    both = both.reshape(block, 16, own).swapaxes(0, 1)
    both = lax.all_to_all(both, tensor, split_axis=0, concat_axis=0, tiled=True)
    prompt_rows, state = both[:, :count], both[:, count:]

    def turn_rows(turn):
        return jnp.concatenate([prompt_rows[:, turn * span : (turn + 1) * span], state], axis=1)

    rows = turn_rows(0)
    pair = core_pair(rows.reshape(-1, own))
    mine = [[pair, *in_turn([(pair, slot) for slot in (1, 2, 3)], ring, 1)] for ring in cross]
    gate_up = [share_cores([gates[0], *results[:3]]) for gates, results in zip(packed, weights)]
    down = [share_cores([downs[0], *results[3:]]) for downs, results in zip(packed_down, weights)]

    outs = []
    for turn in range(STEPS):
        if turn > 0:
            rows = turn_rows(turn)
            mine = gather_rows(rows.reshape(-1, own))
        update = block_update(mine, wheres, gate_up, down).reshape(rows.shape)
        outs.append(update[:, :span].astype(jnp.bfloat16))
        state = (state.astype(jnp.float32) + update[:, span:]).astype(jnp.bfloat16)

    both = jnp.concatenate(outs + [state], axis=1)
    both = lax.all_to_all(both, tensor, split_axis=0, concat_axis=0, tiled=True)
    both = both.swapaxes(0, 1).reshape(block, 16 * own)
    return both[:count], both[count:]


def solution(mesh):
    fine = Mesh(mesh.devices.reshape(4, 2, 2, 4, 2), ("y", "xl", "xh", "z", "c"))
    fsdp, tensor = ("y", "xl"), ("xh", "z", "c")
    return jax.shard_map(
        shards,
        mesh=fine,
        in_specs=(
            P(tensor, fsdp),
            P(tensor, fsdp),
            P(fsdp + tensor, None),
            P(fsdp + tensor, None),
            P(None, fsdp + tensor),
        ),
        out_specs=(P(tensor, fsdp), P(tensor, fsdp)),
        check_vma=False,
    )
```
